32 devices in a mesh: groups: 2 (over x), hid: 8 (over z, y), wid: 2 (over core).
Axes of the slice: x: 2, y: 2, z: 4, core: 2. Of those that a mesh axis runs over, the one named last changes fastest.
Arguments:
- act_rows: bfloat16 [128, 8192], P(('groups', 'hid'), 'wid'), parts along dimension 0, may hold values from -6 to 6
- gate_up_mask: int32 [128, 224], P(('groups', 'wid'), 'hid'), parts along dimension 0, may hold values from 0 to 1, as said below
- gate_blocks: bfloat16 [65536, 1024], P(('groups', 'wid'), 'hid'), parts along dimension 0, may hold values from -0.09375 to 0.09375
- up_blocks: bfloat16 [65536, 1024], P(('groups', 'wid'), 'hid'), parts along dimension 0, may hold values from -0.09375 to 0.09375
- down_mask: int32 [448, 64], P(('groups', 'hid'), 'wid'), parts along dimension 0, may hold values from 0 to 1, as said below
- down_blocks: bfloat16 [262144, 256], P(('groups', 'hid'), 'wid'), parts along dimension 0, may hold values from -0.046875 to 0.046875
Outputs:
- layer_out: bfloat16 [128, 8192], P(('groups', 'hid'), 'wid'), parts along dimension 0
The draws below stay inside these ranges and needn't reach their ends.
There are 2 independent parts, one for each index of `groups`. The reference program is written for one: setup_inputs(seed, part) draws one part's arguments, and reference() takes and returns one part's arrays. A program takes and returns all parts, laid end to end along the dimension named above; each array names one. Nothing has to cross between parts.
Inputs may be any that keep to these rules, and one draw needn't show every extreme that they name: `gate_up_mask`: each device tile of the mask (32 by 28 entries) holds at most 128 set entries, and some tile holds exactly 128. `down_mask`: each device tile of the mask (28 by 32 entries) holds at most 128 set entries, and some tile holds exactly 128.
All inputs are finite; a program needn't handle non-finite values.
Results may differ from the reference program's by a relative error of at most 0.005.
Values may be sent and summed in bfloat16 or wider, within the bound.
A program may use at most 128 MiB of HBM per device.

```python
import jax
import jax.numpy as jnp
from jax import lax

D = 8192
FF = 28672
BLK = 128
CAP = 128
ROWS = 64
N_HID = 8
N_WID = 2


def tile_mask(key, tile_rows, tile_cols, tiles_down, tiles_across):
    tile_count = tiles_down * tiles_across
    cell_count = tile_rows * tile_cols
    key_count, key_forced, key_order = jax.random.split(key, 3)
    counts = jax.random.randint(key_count, (tile_count,), CAP - CAP // 4, CAP + 1)
    forced = jax.random.randint(key_forced, (), 0, tile_count)
    counts = jnp.where(jnp.arange(tile_count) == forced, CAP, counts)
    scores = jax.random.randint(key_order, (tile_count, cell_count), 0, 2 ** 20) * cell_count + jnp.arange(cell_count)[None, :]
    rank_order = jnp.argsort(jnp.argsort(scores, axis=1), axis=1)
    occupied = (rank_order < counts[:, None]).astype(jnp.int32)
    occupied = occupied.reshape(tiles_down, tiles_across, tile_rows, tile_cols).transpose(0, 2, 1, 3)
    return occupied.reshape(tiles_down * tile_rows, tiles_across * tile_cols)


def draw_gate_up_mask(key, part):
    key = jax.random.fold_in(key, 11)
    return tile_mask(key, D // BLK // N_WID, FF // BLK // N_HID, N_WID, N_HID)


def draw_down_mask(key, part):
    key = jax.random.fold_in(key, 23)
    return tile_mask(key, FF // BLK // N_HID, D // BLK // N_WID, N_HID, N_WID)


def levels(own_key, shape, shards, low, top_value):
    def one(axis_at, shards_of):
        heights = jax.random.uniform(jax.random.fold_in(jax.random.fold_in(own_key, 6), axis_at), (shards_of,), jnp.float32, low / len(shards), top_value / len(shards))
        return jnp.repeat(jnp.exp(heights), shape[axis_at] // shards_of).reshape((-1,) + (1,) * (len(shape) - axis_at - 1))

    factor_of = one(*shards[0])
    for cut in shards[1:]:
        factor_of = factor_of * one(*cut)
    return factor_of


def noise(rng, extent, scale, limit, cuts=(), held_as=jnp.bfloat16):
    array = scale * jax.random.normal(rng, extent, jnp.float32)
    if cuts:
        array = array * levels(rng, extent, cuts, -0.22, 0.18)
    return jnp.clip(array, -limit, limit).astype(held_as)


def setup_inputs(seed: int = 0, part: int = 0) -> dict:
    key_of = jax.random.split(jax.random.key(seed), 7)
    own_keys = jax.random.split(jax.random.fold_in(key_of[6], part), 7)
    return {
        "act_rows": noise(own_keys[0], (ROWS, D), 1.0, 6.0, ((0, 8), (1, 2))),
        "gate_up_mask": draw_gate_up_mask(jax.random.fold_in(jax.random.fold_in(key_of[6], part), 71), part),
        "gate_blocks": noise(own_keys[2], (N_WID * CAP * BLK, N_HID * BLK), (D // 2) ** -0.5, 0.09375, ((0, 2), (1, 8))),
        "up_blocks": noise(own_keys[3], (N_WID * CAP * BLK, N_HID * BLK), (D // 2) ** -0.5, 0.09375, ((0, 2), (1, 8))),
        "down_mask": draw_down_mask(jax.random.fold_in(jax.random.fold_in(key_of[6], part), 71), part),
        "down_blocks": noise(own_keys[5], (N_HID * CAP * BLK, N_WID * BLK), (FF // 2) ** -0.5, 0.046875, ((0, 8), (1, 2))),
    }


def unpack_tile(packed, mask_tile):
    tile_rows, tile_cols = mask_tile.shape
    flattened = mask_tile.reshape(-1).astype(jnp.int32)
    slot_index = jnp.clip(jnp.cumsum(flattened).astype(jnp.int32) - 1, 0, CAP - 1).astype(jnp.int32)
    stacked = packed.reshape(CAP, BLK, BLK)
    picked = jnp.take(stacked, slot_index, axis=0)
    picked = jnp.where((flattened == 1)[:, None, None], picked, jnp.zeros_like(picked))
    return picked.reshape(tile_rows, tile_cols, BLK, BLK).transpose(0, 2, 1, 3).reshape(tile_rows * BLK, tile_cols * BLK)


def reference(act_rows, gate_up_mask, gate_blocks, up_blocks, down_mask, down_blocks):
    tile_rows = D // BLK // N_WID
    tile_cols = FF // BLK // N_HID

    def column_tile(total, index):
        index = index.astype(jnp.int32)
        mask_col = (index * tile_cols).astype(jnp.int32)
        pack_row = (index * (CAP * BLK)).astype(jnp.int32)
        pack_col = (index * BLK).astype(jnp.int32)
        gate_parts = []
        up_parts = []
        down_parts = []
        for side in range(N_WID):
            side_rows = jnp.asarray(side * tile_rows, dtype=jnp.int32)
            side_pack = jnp.asarray(side * CAP * BLK, dtype=jnp.int32)
            side_col = jnp.asarray(side * BLK, dtype=jnp.int32)
            mask_tile = lax.dynamic_slice(gate_up_mask, (side_rows, mask_col), (tile_rows, tile_cols))
            gate_pack = lax.dynamic_slice(gate_blocks, (side_pack, pack_col), (CAP * BLK, BLK))
            up_pack = lax.dynamic_slice(up_blocks, (side_pack, pack_col), (CAP * BLK, BLK))
            gate_parts.append(unpack_tile(gate_pack, mask_tile))
            up_parts.append(unpack_tile(up_pack, mask_tile))
            down_tile = lax.dynamic_slice(down_mask, (mask_col, side_rows), (tile_cols, tile_rows))
            down_pack = lax.dynamic_slice(down_blocks, (pack_row, side_col), (CAP * BLK, BLK))
            down_parts.append(unpack_tile(down_pack, down_tile))
        gate_dense = jnp.concatenate(gate_parts, axis=0)
        up_dense = jnp.concatenate(up_parts, axis=0)
        down_dense = jnp.concatenate(down_parts, axis=1)
        gate = jnp.dot(act_rows, gate_dense, preferred_element_type=jnp.float32)
        upward = jnp.dot(act_rows, up_dense, preferred_element_type=jnp.float32)
        hidden = (jax.nn.silu(gate) * upward).astype(jnp.bfloat16)
        return total + jnp.dot(hidden, down_dense, preferred_element_type=jnp.float32), None

    start_total = jnp.zeros((act_rows.shape[0], D), jnp.float32)
    total, _ = lax.scan(column_tile, start_total, jnp.arange(N_HID, dtype=jnp.int32))
    return total.astype(jnp.bfloat16)
```

```python
import functools

import jax
import jax.numpy as jnp
from jax import lax
from jax.experimental import pallas as pl
from jax.experimental.pallas import tpu as pltpu
from jax.sharding import PartitionSpec as P

F32 = jnp.float32
BF16 = jnp.bfloat16
MESH = pl.DeviceIdType.MESH


def iota(shape, dim):
    return lax.broadcasted_iota(jnp.int32, shape, dim)


def dot(a, b):
    return jnp.dot(a, b, preferred_element_type=F32)


def fill_table(mask_ref, table_ref):
    rows, cols = mask_ref.shape
    cap = table_ref.shape[1]
    mask = mask_ref[...].astype(F32)
    mb = mask.astype(BF16)
    lower = (iota((rows, rows), 1) < iota((rows, rows), 0)).astype(F32).astype(BF16)
    upper = (iota((cols, cols), 0) < iota((cols, cols), 1)).astype(F32).astype(BF16)
    upper_wide = (iota((cols, cap), 0) < iota((cols, cap), 1)).astype(F32).astype(BF16)
    same_wide = (iota((cols, cap), 0) == iota((cols, cap), 1)).astype(F32).astype(BF16)
    rank = dot(lower, mb)
    count = dot(jnp.ones((8, rows), BF16), mb).astype(BF16)
    start = dot(count, upper)[0:1]
    start_wide = dot(count, upper_wide)[0:1]
    count_wide = dot(count, same_wide)[0:1]
    in_row = dot(mb, upper)
    row_start = dot(lower, jnp.sum(mask, axis=1, keepdims=True).astype(BF16) * jnp.ones((1, cols), BF16))
    slot = in_row + row_start
    position = jnp.where(mask > 0, rank + start, -1.0)
    packed = slot + float(cap) * (iota((rows, cols), 0).astype(F32) * 2.0 + jnp.where(rank > 0, 1.0, 0.0))
    lane = iota((rows, cap), 1).astype(F32)
    total = jnp.zeros((rows, cap), F32)
    for c in range(cols):
        total += jnp.where(position[:, c : c + 1] == lane, packed[:, c : c + 1], 0.0)
    found = jnp.sum(total, axis=0, keepdims=True).astype(jnp.int32)
    slot_at = found % cap
    rest = found // cap
    table_ref[0:1, :] = slot_at
    table_ref[1:2, :] = rest // 2
    table_ref[2:3, :] = rest % 2
    table_ref[3:4, :] = jnp.maximum(start_wide + count_wide - 1.0, 0.0).astype(jnp.int32)
    table_ref[4:5, :] = jnp.where(count_wide > 0, 1.0, 0.0).astype(jnp.int32)


def entry(table, row, k, size):
    return jnp.clip(table[row, k], 0, size - 1)


def sparse_product(table, x_ref, w_ref, sums_ref, unroll):
    cap, rows, block = sums_ref.shape

    def step(k, total):
        keep = table[2, k].astype(F32)
        total = total * keep + dot(x_ref[entry(table, 1, k, x_ref.shape[0])], w_ref[entry(table, 0, k, cap)])
        sums_ref[k] = total
        return total

    lax.fori_loop(0, cap, step, jnp.zeros((rows, block), F32), unroll=unroll)


def kernel(
    n_hid, act_ref, gu_mask_ref, gate_hbm, up_hbm, down_mask_ref, down_hbm, out_ref,
    gate_w, up_w, down_w, gathered, wide, x, gu_tab_v, down_tab_v, gu_tab, down_tab,
    sums, gate_own, up_own, gate_send, up_send, gate_recv, up_recv, hidden,
    part, y_send, y_recv, z_send, z_recv,
    w_sem, tab_sem, ag_send, ag_recv, fw_send, wid_send, wid_recv, ry_send, ry_recv, rz_send, rz_recv,
):
    ny = 2
    nz = n_hid // ny
    me = lax.axis_index("hid")
    z, y = me // ny, me % ny
    core = lax.axis_index("wid")
    y_peer = z * ny + (1 - y)
    own_rows, width = act_ref.shape
    block = x.shape[2]
    k_blocks = x.shape[0]
    ff_blocks = hidden.shape[0]
    rows = x.shape[1]

    def z_hid(j):
        return lax.rem(z + j, nz) * ny + y

    def from_hid(j):
        return lax.rem(z + nz - j, nz) * ny + y

    loads = [
        pltpu.make_async_copy(src, dst, w_sem.at[i])
        for i, (src, dst) in enumerate(((gate_hbm, gate_w), (up_hbm, up_w), (down_hbm, down_w)))
    ]
    for load in loads:
        load.start()

    barrier = pltpu.get_barrier_semaphore()
    for j in range(1, nz):
        pl.semaphore_signal(barrier, inc=1, device_id={"hid": z_hid(j)}, device_id_type=MESH)
    pl.semaphore_signal(barrier, inc=1, device_id={"hid": y_peer}, device_id_type=MESH)
    pl.semaphore_signal(barrier, inc=1, device_id={"wid": 1 - core}, device_id_type=MESH)

    for b in range(k_blocks):
        wide[b, 0:own_rows, :] = act_ref[:, b * block : (b + 1) * block].astype(F32)
    gathered[me] = wide[:, 0:own_rows, :].reshape(k_blocks * own_rows, block).astype(BF16)

    pl.semaphore_wait(barrier, nz + 1)

    def send_act(slot, target, send_sem):
        return pltpu.make_async_remote_copy(
            src_ref=gathered.at[slot], dst_ref=gathered.at[slot], send_sem=send_sem,
            recv_sem=ag_recv.at[slot], device_id={"hid": target}, device_id_type=MESH)

    sends = []
    copy = send_act(me, y_peer, fw_send.at[0])
    copy.start()
    sends.append(copy)
    for j in range(1, nz):
        copy = send_act(me, z_hid(j), ag_send.at[j])
        copy.start()
        sends.append(copy)

    fill_table(gu_mask_ref, gu_tab_v)
    gu_copy = pltpu.make_async_copy(gu_tab_v, gu_tab, tab_sem.at[0])
    gu_copy.start()

    for j in range(1, nz):
        slot = from_hid(j)
        send_act(slot, y_peer, fw_send.at[j]).wait_recv()
        copy = send_act(slot, y_peer, fw_send.at[j])
        copy.start()
        sends.append(copy)

    fill_table(down_mask_ref, down_tab_v)
    down_copy = pltpu.make_async_copy(down_tab_v, down_tab, tab_sem.at[1])
    down_copy.start()

    for j in range(nz):
        slot = lax.rem(z + nz - j, nz) * ny + (1 - y)
        send_act(slot, y_peer, fw_send.at[j]).wait_recv()
    for p in range(n_hid):
        wide[:, p * own_rows : (p + 1) * own_rows, :] = (
            gathered[p].astype(F32).reshape(k_blocks, own_rows, block))
    x[...] = wide[...].astype(BF16)

    gu_copy.wait()

    def to_wid(src, dst, i):
        return pltpu.make_async_remote_copy(
            src_ref=src, dst_ref=dst, send_sem=wid_send.at[i], recv_sem=wid_recv.at[i],
            device_id={"wid": 1 - core}, device_id_type=MESH)

    def half(load, w, own, send, recv, i):
        load.wait()
        sparse_product(gu_tab, x, w, sums, 8)

        def column(c, _):
            value = sums[entry(gu_tab, 3, c, sums.shape[0])] * gu_tab[4, c].astype(F32)
            own[c] = value
            send[c] = value.astype(BF16)
            return 0

        lax.fori_loop(0, ff_blocks, column, 0)
        copy = to_wid(send, recv, i)
        copy.start()
        return copy

    gate_copy = half(loads[0], gate_w, gate_own, gate_send, gate_recv, 0)
    up_copy = half(loads[1], up_w, up_own, up_send, up_recv, 1)
    gate_copy.wait_recv()
    up_copy.wait_recv()

    def activate(c, _):
        gate = gate_own[c] + gate_recv[c].astype(F32)
        up = up_own[c] + up_recv[c].astype(F32)
        hidden[c] = (gate / (1.0 + jnp.exp(-gate)) * up).astype(BF16)
        return 0

    lax.fori_loop(0, ff_blocks, activate, 0)

    down_copy.wait()
    loads[2].wait()
    sparse_product(down_tab, hidden, down_w, sums, 8)

    for c in range(k_blocks):
        value = sums[entry(down_tab, 3, c, sums.shape[0])] * down_tab[4, c].astype(F32)
        for p in range(n_hid):
            part[p, c * own_rows : (c + 1) * own_rows, :] = value[p * own_rows : (p + 1) * own_rows]

    def to_y(j):
        return pltpu.make_async_remote_copy(
            src_ref=y_send.at[j], dst_ref=y_recv.at[j], send_sem=ry_send.at[j],
            recv_sem=ry_recv.at[j], device_id={"hid": y_peer}, device_id_type=MESH)

    def to_z(j):
        return pltpu.make_async_remote_copy(
            src_ref=z_send.at[j], dst_ref=z_recv.at[j], send_sem=rz_send.at[j],
            recv_sem=rz_recv.at[j], device_id={"hid": z_hid(j)}, device_id_type=MESH)

    order = list(range(1, nz)) + [0]
    for j in order:
        y_send[j] = part[lax.rem(z + j, nz) * ny + (1 - y)].astype(BF16)
        copy = to_y(j)
        copy.start()
        sends.append(copy)
    for j in range(1, nz):
        to_y(j).wait_recv()
        z_send[j] = (part[z_hid(j)] + y_recv[j].astype(F32)).astype(BF16)
        copy = to_z(j)
        copy.start()
        sends.append(copy)
    to_y(0).wait_recv()
    total = part[me] + y_recv[0].astype(F32)
    for j in range(1, nz):
        to_z(j).wait_recv()
        total += z_recv[j].astype(F32)
    for b in range(k_blocks):
        out_ref[:, b * block : (b + 1) * block] = total[b * own_rows : (b + 1) * own_rows].astype(BF16)

    for copy in sends:
        copy.wait_send()
    gate_copy.wait_send()
    up_copy.wait_send()


def per_device(n_hid, act_rows, gate_up_mask, gate_blocks, up_blocks, down_mask, down_blocks):
    own_rows, width = act_rows.shape
    block = gate_blocks.shape[1]
    cap = gate_blocks.shape[0] // block
    k_blocks, ff_blocks = gate_up_mask.shape
    rows = own_rows * n_hid
    nz = n_hid // 2
    piece = (k_blocks * own_rows, block)
    stacked = (cap, block, block)
    vmem = pl.BlockSpec(memory_space=pltpu.VMEM)
    hbm = pl.BlockSpec(memory_space=pl.ANY)
    dma = pltpu.SemaphoreType.DMA
    return pl.pallas_call(
        functools.partial(kernel, n_hid),
        out_shape=jax.ShapeDtypeStruct(act_rows.shape, BF16),
        in_specs=[vmem, vmem, hbm, hbm, vmem, hbm],
        out_specs=vmem,
        scratch_shapes=[
            pltpu.VMEM(stacked, BF16), pltpu.VMEM(stacked, BF16), pltpu.VMEM(stacked, BF16),
            pltpu.VMEM((n_hid,) + piece, BF16),
            pltpu.VMEM((k_blocks, rows, block), F32),
            pltpu.VMEM((k_blocks, rows, block), BF16),
            pltpu.VMEM((8, cap), jnp.int32), pltpu.VMEM((8, cap), jnp.int32),
            pltpu.SMEM((8, cap), jnp.int32), pltpu.SMEM((8, cap), jnp.int32),
            pltpu.VMEM((cap, rows, block), F32),
            pltpu.VMEM((ff_blocks, rows, block), F32), pltpu.VMEM((ff_blocks, rows, block), F32),
            pltpu.VMEM((ff_blocks, rows, block), BF16), pltpu.VMEM((ff_blocks, rows, block), BF16),
            pltpu.VMEM((ff_blocks, rows, block), BF16), pltpu.VMEM((ff_blocks, rows, block), BF16),
            pltpu.VMEM((ff_blocks, rows, block), BF16),
            pltpu.VMEM((n_hid,) + piece, F32),
            pltpu.VMEM((nz,) + piece, BF16), pltpu.VMEM((nz,) + piece, BF16),
            pltpu.VMEM((nz,) + piece, BF16), pltpu.VMEM((nz,) + piece, BF16),
            dma((3,)), dma((2,)), dma((nz,)), dma((n_hid,)), dma((nz,)),
            dma((2,)), dma((2,)), dma((nz,)), dma((nz,)), dma((nz,)), dma((nz,)),
        ],
        compiler_params=pltpu.CompilerParams(
            collective_id=0, has_side_effects=True, vmem_limit_bytes=60 * 2 ** 20),
        cost_estimate=pl.CostEstimate(
            flops=6 * cap * rows * block * block, bytes_accessed=6 * cap * block * block, transcendentals=0),
    )(
        act_rows, gate_up_mask, gate_blocks.reshape(stacked), up_blocks.reshape(stacked),
        down_mask, down_blocks.reshape(stacked),
    )


def solution(mesh):
    in_specs = (
        P(("groups", "hid"), "wid"),
        P(("groups", "wid"), "hid"),
        P(("groups", "wid"), "hid"),
        P(("groups", "wid"), "hid"),
        P(("groups", "hid"), "wid"),
        P(("groups", "hid"), "wid"),
    )
    out_specs = P(("groups", "hid"), "wid")
    return jax.shard_map(
        functools.partial(per_device, mesh.shape["hid"]),
        mesh=mesh, in_specs=in_specs, out_specs=out_specs, check_vma=False,
    )
```

```python
import functools

import jax
import jax.numpy as jnp
from jax import lax
from jax.experimental import pallas as pl
from jax.experimental.pallas import tpu as pltpu
from jax.sharding import PartitionSpec as P

F32 = jnp.float32
BF16 = jnp.bfloat16
MESH = pl.DeviceIdType.MESH


def iota(shape, dim):
    return lax.broadcasted_iota(jnp.int32, shape, dim)


def dot(a, b):
    return jnp.dot(a, b, preferred_element_type=F32)


def fill_table(mask_ref, table_ref):
    rows, cols = mask_ref.shape
    cap = table_ref.shape[1]
    mask = mask_ref[...].astype(F32)
    mb = mask.astype(BF16)
    lower = (iota((rows, rows), 1) < iota((rows, rows), 0)).astype(F32).astype(BF16)
    upper = (iota((cols, cols), 0) < iota((cols, cols), 1)).astype(F32).astype(BF16)
    upper_wide = (iota((cols, cap), 0) < iota((cols, cap), 1)).astype(F32).astype(BF16)
    same_wide = (iota((cols, cap), 0) == iota((cols, cap), 1)).astype(F32).astype(BF16)
    rank = dot(lower, mb)
    count = dot(jnp.ones((8, rows), BF16), mb).astype(BF16)
    start = dot(count, upper)[0:1]
    start_wide = dot(count, upper_wide)[0:1]
    count_wide = dot(count, same_wide)[0:1]
    in_row = dot(mb, upper)
    row_start = dot(lower, jnp.sum(mask, axis=1, keepdims=True).astype(BF16) * jnp.ones((1, cols), BF16))
    slot = in_row + row_start
    position = jnp.where(mask > 0, rank + start, -1.0)
    packed = slot + float(cap) * (iota((rows, cols), 0).astype(F32) * 2.0 + jnp.where(rank > 0, 1.0, 0.0))
    lane = iota((rows, cap), 1).astype(F32)
    total = jnp.zeros((rows, cap), F32)
    for c in range(cols):
        total += jnp.where(position[:, c : c + 1] == lane, packed[:, c : c + 1], 0.0)
    found = jnp.sum(total, axis=0, keepdims=True).astype(jnp.int32)
    slot_at = found % cap
    rest = found // cap
    table_ref[0:1, :] = slot_at
    table_ref[1:2, :] = rest // 2
    table_ref[2:3, :] = rest % 2
    table_ref[3:4, :] = jnp.maximum(start_wide + count_wide - 1.0, 0.0).astype(jnp.int32)
    table_ref[4:5, :] = jnp.where(count_wide > 0, 1.0, 0.0).astype(jnp.int32)


def entry(table, row, k, size):
    return jnp.clip(table[row, k], 0, size - 1)


def sparse_product(table, x_ref, w_ref, sums_ref, unroll):
    cap, rows, block = sums_ref.shape

    def step(k, total):
        keep = table[2, k].astype(F32)
        total = total * keep + dot(x_ref[entry(table, 1, k, x_ref.shape[0])], w_ref[entry(table, 0, k, cap)])
        sums_ref[k] = total
        return total

    lax.fori_loop(0, cap, step, jnp.zeros((rows, block), F32), unroll=unroll)


def kernel(
    n_hid, act_ref, gu_mask_ref, gate_hbm, up_hbm, down_mask_ref, down_hbm, out_ref,
    gate_w, up_w, down_w, gathered, wide, x, gu_tab_v, down_tab_v, gu_tab, down_tab,
    sums, gate_own, up_own, gate_send, up_send, gate_recv, up_recv, hidden,
    part, y_send, y_recv, z_send, z_recv,
    w_sem, tab_sem, ag_send, ag_recv, fw_send, wid_send, wid_recv, ry_send, ry_recv, rz_send, rz_recv,
):
    ny = 2
    nz = n_hid // ny
    me = lax.axis_index("hid")
    z, y = me // ny, me % ny
    core = lax.axis_index("wid")
    y_peer = z * ny + (1 - y)
    own_rows, width = act_ref.shape
    block = x.shape[2]
    k_blocks = x.shape[0]
    ff_blocks = hidden.shape[0]
    rows = x.shape[1]

    def z_hid(j):
        return lax.rem(z + j, nz) * ny + y

    def from_hid(j):
        return lax.rem(z + nz - j, nz) * ny + y

    loads = [
        pltpu.make_async_copy(src, dst, w_sem.at[i])
        for i, (src, dst) in enumerate(((gate_hbm, gate_w), (up_hbm, up_w), (down_hbm, down_w)))
    ]
    for load in loads:
        load.start()

    barrier = pltpu.get_barrier_semaphore()
    for j in range(1, nz):
        pl.semaphore_signal(barrier, inc=1, device_id={"hid": z_hid(j)}, device_id_type=MESH)
    pl.semaphore_signal(barrier, inc=1, device_id={"hid": y_peer}, device_id_type=MESH)
    pl.semaphore_signal(barrier, inc=1, device_id={"wid": 1 - core}, device_id_type=MESH)

    for b in range(k_blocks):
        wide[b, 0:own_rows, :] = act_ref[:, b * block : (b + 1) * block].astype(F32)
    gathered[me] = wide[:, 0:own_rows, :].reshape(k_blocks * own_rows, block).astype(BF16)

    pl.semaphore_wait(barrier, nz + 1)

    def send_act(slot, target, send_sem):
        return pltpu.make_async_remote_copy(
            src_ref=gathered.at[slot], dst_ref=gathered.at[slot], send_sem=send_sem,
            recv_sem=ag_recv.at[slot], device_id={"hid": target}, device_id_type=MESH)

    sends = []
    copy = send_act(me, y_peer, fw_send.at[0])
    copy.start()
    sends.append(copy)
    for j in range(1, nz):
        copy = send_act(me, z_hid(j), ag_send.at[j])
        copy.start()
        sends.append(copy)

    fill_table(gu_mask_ref, gu_tab_v)
    gu_copy = pltpu.make_async_copy(gu_tab_v, gu_tab, tab_sem.at[0])
    gu_copy.start()

    for j in range(1, nz):
        slot = from_hid(j)
        send_act(slot, y_peer, fw_send.at[j]).wait_recv()
        copy = send_act(slot, y_peer, fw_send.at[j])
        copy.start()
        sends.append(copy)

    fill_table(down_mask_ref, down_tab_v)
    down_copy = pltpu.make_async_copy(down_tab_v, down_tab, tab_sem.at[1])
    down_copy.start()

    for j in range(nz):
        slot = lax.rem(z + nz - j, nz) * ny + (1 - y)
        send_act(slot, y_peer, fw_send.at[j]).wait_recv()
    for p in range(n_hid):
        wide[:, p * own_rows : (p + 1) * own_rows, :] = (
            gathered[p].astype(F32).reshape(k_blocks, own_rows, block))
    x[...] = wide[...].astype(BF16)

    gu_copy.wait()

    def to_wid(src, dst, i):
        return pltpu.make_async_remote_copy(
            src_ref=src, dst_ref=dst, send_sem=wid_send.at[i], recv_sem=wid_recv.at[i],
            device_id={"wid": 1 - core}, device_id_type=MESH)

    def half(load, w, own, send, recv, i):
        load.wait()
        sparse_product(gu_tab, x, w, sums, 128)

        def column(c, _):
            value = sums[entry(gu_tab, 3, c, sums.shape[0])] * gu_tab[4, c].astype(F32)
            own[c] = value
            send[c] = value.astype(BF16)
            return 0

        for c in range(ff_blocks):
            column(c, 0)
        copy = to_wid(send, recv, i)
        copy.start()
        return copy

    gate_copy = half(loads[0], gate_w, gate_own, gate_send, gate_recv, 0)
    up_copy = half(loads[1], up_w, up_own, up_send, up_recv, 1)
    gate_copy.wait_recv()
    up_copy.wait_recv()

    def activate(c, _):
        gate = gate_own[c] + gate_recv[c].astype(F32)
        up = up_own[c] + up_recv[c].astype(F32)
        hidden[c] = (gate / (1.0 + jnp.exp(-gate)) * up).astype(BF16)
        return 0

    for c in range(ff_blocks):
        activate(c, 0)

    down_copy.wait()
    loads[2].wait()
    sparse_product(down_tab, hidden, down_w, sums, 128)

    for c in range(k_blocks):
        value = sums[entry(down_tab, 3, c, sums.shape[0])] * down_tab[4, c].astype(F32)
        for p in range(n_hid):
            part[p, c * own_rows : (c + 1) * own_rows, :] = value[p * own_rows : (p + 1) * own_rows]

    def to_y(j):
        return pltpu.make_async_remote_copy(
            src_ref=y_send.at[j], dst_ref=y_recv.at[j], send_sem=ry_send.at[j],
            recv_sem=ry_recv.at[j], device_id={"hid": y_peer}, device_id_type=MESH)

    def to_z(j):
        return pltpu.make_async_remote_copy(
            src_ref=z_send.at[j], dst_ref=z_recv.at[j], send_sem=rz_send.at[j],
            recv_sem=rz_recv.at[j], device_id={"hid": z_hid(j)}, device_id_type=MESH)

    order = list(range(1, nz)) + [0]
    for j in order:
        y_send[j] = part[lax.rem(z + j, nz) * ny + (1 - y)].astype(BF16)
        copy = to_y(j)
        copy.start()
        sends.append(copy)
    for j in range(1, nz):
        to_y(j).wait_recv()
        z_send[j] = (part[z_hid(j)] + y_recv[j].astype(F32)).astype(BF16)
        copy = to_z(j)
        copy.start()
        sends.append(copy)
    to_y(0).wait_recv()
    total = part[me] + y_recv[0].astype(F32)
    for j in range(1, nz):
        to_z(j).wait_recv()
        total += z_recv[j].astype(F32)
    for b in range(k_blocks):
        out_ref[:, b * block : (b + 1) * block] = total[b * own_rows : (b + 1) * own_rows].astype(BF16)

    for copy in sends:
        copy.wait_send()
    gate_copy.wait_send()
    up_copy.wait_send()


def per_device(n_hid, act_rows, gate_up_mask, gate_blocks, up_blocks, down_mask, down_blocks):
    own_rows, width = act_rows.shape
    block = gate_blocks.shape[1]
    cap = gate_blocks.shape[0] // block
    k_blocks, ff_blocks = gate_up_mask.shape
    rows = own_rows * n_hid
    nz = n_hid // 2
    piece = (k_blocks * own_rows, block)
    stacked = (cap, block, block)
    vmem = pl.BlockSpec(memory_space=pltpu.VMEM)
    hbm = pl.BlockSpec(memory_space=pl.ANY)
    dma = pltpu.SemaphoreType.DMA
    return pl.pallas_call(
        functools.partial(kernel, n_hid),
        out_shape=jax.ShapeDtypeStruct(act_rows.shape, BF16),
        in_specs=[vmem, vmem, hbm, hbm, vmem, hbm],
        out_specs=vmem,
        scratch_shapes=[
            pltpu.VMEM(stacked, BF16), pltpu.VMEM(stacked, BF16), pltpu.VMEM(stacked, BF16),
            pltpu.VMEM((n_hid,) + piece, BF16),
            pltpu.VMEM((k_blocks, rows, block), F32),
            pltpu.VMEM((k_blocks, rows, block), BF16),
            pltpu.VMEM((8, cap), jnp.int32), pltpu.VMEM((8, cap), jnp.int32),
            pltpu.SMEM((8, cap), jnp.int32), pltpu.SMEM((8, cap), jnp.int32),
            pltpu.VMEM((cap, rows, block), F32),
            pltpu.VMEM((ff_blocks, rows, block), F32), pltpu.VMEM((ff_blocks, rows, block), F32),
            pltpu.VMEM((ff_blocks, rows, block), BF16), pltpu.VMEM((ff_blocks, rows, block), BF16),
            pltpu.VMEM((ff_blocks, rows, block), BF16), pltpu.VMEM((ff_blocks, rows, block), BF16),
            pltpu.VMEM((ff_blocks, rows, block), BF16),
            pltpu.VMEM((n_hid,) + piece, F32),
            pltpu.VMEM((nz,) + piece, BF16), pltpu.VMEM((nz,) + piece, BF16),
            pltpu.VMEM((nz,) + piece, BF16), pltpu.VMEM((nz,) + piece, BF16),
            dma((3,)), dma((2,)), dma((nz,)), dma((n_hid,)), dma((nz,)),
            dma((2,)), dma((2,)), dma((nz,)), dma((nz,)), dma((nz,)), dma((nz,)),
        ],
        compiler_params=pltpu.CompilerParams(
            collective_id=0, has_side_effects=True, vmem_limit_bytes=60 * 2 ** 20),
        cost_estimate=pl.CostEstimate(
            flops=6 * cap * rows * block * block, bytes_accessed=6 * cap * block * block, transcendentals=0),
    )(
        act_rows, gate_up_mask, gate_blocks.reshape(stacked), up_blocks.reshape(stacked),
        down_mask, down_blocks.reshape(stacked),
    )


def solution(mesh):
    in_specs = (
        P(("groups", "hid"), "wid"),
        P(("groups", "wid"), "hid"),
        P(("groups", "wid"), "hid"),
        P(("groups", "wid"), "hid"),
        P(("groups", "hid"), "wid"),
        P(("groups", "hid"), "wid"),
    )
    out_specs = P(("groups", "hid"), "wid")
    return jax.shard_map(
        functools.partial(per_device, mesh.shape["hid"]),
        mesh=mesh, in_specs=in_specs, out_specs=out_specs, check_vma=False,
    )
```

```python
import functools

import jax
import jax.numpy as jnp
from jax import lax
from jax.experimental import pallas as pl
from jax.experimental.pallas import tpu as pltpu
from jax.sharding import PartitionSpec as P

F32 = jnp.float32
BF16 = jnp.bfloat16
MESH = pl.DeviceIdType.MESH


def iota(shape, dim):
    return lax.broadcasted_iota(jnp.int32, shape, dim)


def dot(a, b):
    return jnp.dot(a, b, preferred_element_type=F32)


def fill_table(mask_ref, table_ref):
    rows, cols = mask_ref.shape
    cap = table_ref.shape[1]
    mask = mask_ref[...].astype(F32)
    mb = mask.astype(BF16)
    lower = (iota((rows, rows), 1) < iota((rows, rows), 0)).astype(F32).astype(BF16)
    upper = (iota((cols, cols), 0) < iota((cols, cols), 1)).astype(F32).astype(BF16)
    upper_wide = (iota((cols, cap), 0) < iota((cols, cap), 1)).astype(F32).astype(BF16)
    same_wide = (iota((cols, cap), 0) == iota((cols, cap), 1)).astype(F32).astype(BF16)
    rank = dot(lower, mb)
    count = dot(jnp.ones((8, rows), BF16), mb).astype(BF16)
    start = dot(count, upper)[0:1]
    start_wide = dot(count, upper_wide)[0:1]
    count_wide = dot(count, same_wide)[0:1]
    in_row = dot(mb, upper)
    row_start = dot(lower, jnp.sum(mask, axis=1, keepdims=True).astype(BF16) * jnp.ones((1, cols), BF16))
    slot = in_row + row_start
    position = jnp.where(mask > 0, rank + start, -1.0)
    packed = slot + float(cap) * (iota((rows, cols), 0).astype(F32) * 2.0 + jnp.where(rank > 0, 1.0, 0.0))
    lane = iota((rows, cap), 1).astype(F32)
    total = jnp.zeros((rows, cap), F32)
    for c in range(cols):
        total += jnp.where(position[:, c : c + 1] == lane, packed[:, c : c + 1], 0.0)
    found = jnp.sum(total, axis=0, keepdims=True).astype(jnp.int32)
    slot_at = found % cap
    rest = found // cap
    table_ref[0:1, :] = slot_at
    table_ref[1:2, :] = rest // 2
    table_ref[2:3, :] = rest % 2
    table_ref[3:4, :] = jnp.maximum(start_wide + count_wide - 1.0, 0.0).astype(jnp.int32)
    table_ref[4:5, :] = jnp.where(count_wide > 0, 1.0, 0.0).astype(jnp.int32)


def entry(table, row, k, size):
    return jnp.clip(table[row, k], 0, size - 1)


def sparse_product(table, x_ref, w_ref, sums_ref, unroll):
    cap, rows, block = sums_ref.shape

    def step(k, total):
        keep = table[2, k].astype(F32)
        total = total * keep + dot(x_ref[entry(table, 1, k, x_ref.shape[0])], w_ref[entry(table, 0, k, cap)])
        sums_ref[k] = total
        return total

    lax.fori_loop(0, cap, step, jnp.zeros((rows, block), F32), unroll=unroll)


def kernel(
    n_hid, act_hbm, gu_mask_hbm, gate_hbm, up_hbm, down_mask_hbm, down_hbm, out_ref,
    act_ref, gu_mask_ref, down_mask_ref, small_sem,
    gate_w, up_w, down_w, gathered, wide, x, gu_tab_v, down_tab_v, gu_tab, down_tab,
    sums, gate_own, up_own, gate_send, up_send, gate_recv, up_recv, hidden,
    part, y_send, y_recv, z_send, z_recv,
    w_sem, tab_sem, ag_send, ag_recv, fw_send, wid_send, wid_recv, ry_send, ry_recv, rz_send, rz_recv,
):
    ny = 2
    nz = n_hid // ny
    me = lax.axis_index("hid")
    z, y = me // ny, me % ny
    core = lax.axis_index("wid")
    y_peer = z * ny + (1 - y)
    own_rows, width = act_ref.shape
    block = x.shape[2]
    k_blocks = x.shape[0]
    ff_blocks = hidden.shape[0]
    rows = x.shape[1]

    def z_hid(j):
        return lax.rem(z + j, nz) * ny + y

    def from_hid(j):
        return lax.rem(z + nz - j, nz) * ny + y

    small = [
        pltpu.make_async_copy(src, dst, small_sem.at[i])
        for i, (src, dst) in enumerate(
            ((act_hbm, act_ref), (gu_mask_hbm, gu_mask_ref), (down_mask_hbm, down_mask_ref)))
    ]
    for load in small:
        load.start()
    loads = [
        pltpu.make_async_copy(src, dst, w_sem.at[i])
        for i, (src, dst) in enumerate(((gate_hbm, gate_w), (up_hbm, up_w), (down_hbm, down_w)))
    ]
    for load in loads:
        load.start()

    barrier = pltpu.get_barrier_semaphore()
    for j in range(1, nz):
        pl.semaphore_signal(barrier, inc=1, device_id={"hid": z_hid(j)}, device_id_type=MESH)
    pl.semaphore_signal(barrier, inc=1, device_id={"hid": y_peer}, device_id_type=MESH)
    pl.semaphore_signal(barrier, inc=1, device_id={"wid": 1 - core}, device_id_type=MESH)

    small[0].wait()
    for b in range(k_blocks):
        wide[b, 0:own_rows, :] = act_ref[:, b * block : (b + 1) * block].astype(F32)
    gathered[me] = wide[:, 0:own_rows, :].reshape(k_blocks * own_rows, block).astype(BF16)

    pl.semaphore_wait(barrier, nz + 1)

    def send_act(slot, target, send_sem):
        return pltpu.make_async_remote_copy(
            src_ref=gathered.at[slot], dst_ref=gathered.at[slot], send_sem=send_sem,
            recv_sem=ag_recv.at[slot], device_id={"hid": target}, device_id_type=MESH)

    sends = []
    copy = send_act(me, y_peer, fw_send.at[0])
    copy.start()
    sends.append(copy)
    for j in range(1, nz):
        copy = send_act(me, z_hid(j), ag_send.at[j])
        copy.start()
        sends.append(copy)

    small[1].wait()
    fill_table(gu_mask_ref, gu_tab_v)
    gu_copy = pltpu.make_async_copy(gu_tab_v, gu_tab, tab_sem.at[0])
    gu_copy.start()

    for j in range(1, nz):
        slot = from_hid(j)
        send_act(slot, y_peer, fw_send.at[j]).wait_recv()
        copy = send_act(slot, y_peer, fw_send.at[j])
        copy.start()
        sends.append(copy)

    small[2].wait()
    fill_table(down_mask_ref, down_tab_v)
    down_copy = pltpu.make_async_copy(down_tab_v, down_tab, tab_sem.at[1])
    down_copy.start()

    for j in range(nz):
        slot = lax.rem(z + nz - j, nz) * ny + (1 - y)
        send_act(slot, y_peer, fw_send.at[j]).wait_recv()
    for p in range(n_hid):
        wide[:, p * own_rows : (p + 1) * own_rows, :] = (
            gathered[p].astype(F32).reshape(k_blocks, own_rows, block))
    x[...] = wide[...].astype(BF16)

    gu_copy.wait()

    def to_wid(src, dst, i):
        return pltpu.make_async_remote_copy(
            src_ref=src, dst_ref=dst, send_sem=wid_send.at[i], recv_sem=wid_recv.at[i],
            device_id={"wid": 1 - core}, device_id_type=MESH)

    def half(load, w, own, send, recv, i):
        load.wait()
        sparse_product(gu_tab, x, w, sums, 128)

        def column(c, _):
            value = sums[entry(gu_tab, 3, c, sums.shape[0])] * gu_tab[4, c].astype(F32)
            own[c] = value
            send[c] = value.astype(BF16)
            return 0

        for c in range(ff_blocks):
            column(c, 0)
        copy = to_wid(send, recv, i)
        copy.start()
        return copy

    gate_copy = half(loads[0], gate_w, gate_own, gate_send, gate_recv, 0)
    up_copy = half(loads[1], up_w, up_own, up_send, up_recv, 1)
    gate_copy.wait_recv()
    up_copy.wait_recv()

    def activate(c, _):
        gate = gate_own[c] + gate_recv[c].astype(F32)
        up = up_own[c] + up_recv[c].astype(F32)
        hidden[c] = (gate / (1.0 + jnp.exp(-gate)) * up).astype(BF16)
        return 0

    for c in range(ff_blocks):
        activate(c, 0)

    down_copy.wait()
    loads[2].wait()
    sparse_product(down_tab, hidden, down_w, sums, 128)

    for c in range(k_blocks):
        value = sums[entry(down_tab, 3, c, sums.shape[0])] * down_tab[4, c].astype(F32)
        for p in range(n_hid):
            part[p, c * own_rows : (c + 1) * own_rows, :] = value[p * own_rows : (p + 1) * own_rows]

    def to_y(j):
        return pltpu.make_async_remote_copy(
            src_ref=y_send.at[j], dst_ref=y_recv.at[j], send_sem=ry_send.at[j],
            recv_sem=ry_recv.at[j], device_id={"hid": y_peer}, device_id_type=MESH)

    def to_z(j):
        return pltpu.make_async_remote_copy(
            src_ref=z_send.at[j], dst_ref=z_recv.at[j], send_sem=rz_send.at[j],
            recv_sem=rz_recv.at[j], device_id={"hid": z_hid(j)}, device_id_type=MESH)

    order = list(range(1, nz)) + [0]
    for j in order:
        y_send[j] = part[lax.rem(z + j, nz) * ny + (1 - y)].astype(BF16)
        copy = to_y(j)
        copy.start()
        sends.append(copy)
    for j in range(1, nz):
        to_y(j).wait_recv()
        z_send[j] = (part[z_hid(j)] + y_recv[j].astype(F32)).astype(BF16)
        copy = to_z(j)
        copy.start()
        sends.append(copy)
    to_y(0).wait_recv()
    total = part[me] + y_recv[0].astype(F32)
    for j in range(1, nz):
        to_z(j).wait_recv()
        total += z_recv[j].astype(F32)
    for b in range(k_blocks):
        out_ref[:, b * block : (b + 1) * block] = total[b * own_rows : (b + 1) * own_rows].astype(BF16)

    for copy in sends:
        copy.wait_send()
    gate_copy.wait_send()
    up_copy.wait_send()


def per_device(n_hid, act_rows, gate_up_mask, gate_blocks, up_blocks, down_mask, down_blocks):
    own_rows, width = act_rows.shape
    block = gate_blocks.shape[1]
    cap = gate_blocks.shape[0] // block
    k_blocks, ff_blocks = gate_up_mask.shape
    rows = own_rows * n_hid
    nz = n_hid // 2
    piece = (k_blocks * own_rows, block)
    stacked = (cap, block, block)
    vmem = pl.BlockSpec(memory_space=pltpu.VMEM)
    hbm = pl.BlockSpec(memory_space=pl.ANY)
    dma = pltpu.SemaphoreType.DMA
    return pl.pallas_call(
        functools.partial(kernel, n_hid),
        out_shape=jax.ShapeDtypeStruct(act_rows.shape, BF16),
        in_specs=[hbm, hbm, hbm, hbm, hbm, hbm],
        out_specs=vmem,
        scratch_shapes=[
            pltpu.VMEM(act_rows.shape, BF16), pltpu.VMEM(gate_up_mask.shape, jnp.int32),
            pltpu.VMEM(down_mask.shape, jnp.int32), dma((3,)),
            pltpu.VMEM(stacked, BF16), pltpu.VMEM(stacked, BF16), pltpu.VMEM(stacked, BF16),
            pltpu.VMEM((n_hid,) + piece, BF16),
            pltpu.VMEM((k_blocks, rows, block), F32),
            pltpu.VMEM((k_blocks, rows, block), BF16),
            pltpu.VMEM((8, cap), jnp.int32), pltpu.VMEM((8, cap), jnp.int32),
            pltpu.SMEM((8, cap), jnp.int32), pltpu.SMEM((8, cap), jnp.int32),
            pltpu.VMEM((cap, rows, block), F32),
            pltpu.VMEM((ff_blocks, rows, block), F32), pltpu.VMEM((ff_blocks, rows, block), F32),
            pltpu.VMEM((ff_blocks, rows, block), BF16), pltpu.VMEM((ff_blocks, rows, block), BF16),
            pltpu.VMEM((ff_blocks, rows, block), BF16), pltpu.VMEM((ff_blocks, rows, block), BF16),
            pltpu.VMEM((ff_blocks, rows, block), BF16),
            pltpu.VMEM((n_hid,) + piece, F32),
            pltpu.VMEM((nz,) + piece, BF16), pltpu.VMEM((nz,) + piece, BF16),
            pltpu.VMEM((nz,) + piece, BF16), pltpu.VMEM((nz,) + piece, BF16),
            dma((3,)), dma((2,)), dma((nz,)), dma((n_hid,)), dma((nz,)),
            dma((2,)), dma((2,)), dma((nz,)), dma((nz,)), dma((nz,)), dma((nz,)),
        ],
        compiler_params=pltpu.CompilerParams(
            collective_id=0, has_side_effects=True, vmem_limit_bytes=60 * 2 ** 20),
        cost_estimate=pl.CostEstimate(
            flops=6 * cap * rows * block * block, bytes_accessed=6 * cap * block * block, transcendentals=0),
    )(
        act_rows, gate_up_mask, gate_blocks.reshape(stacked), up_blocks.reshape(stacked),
        down_mask, down_blocks.reshape(stacked),
    )


def solution(mesh):
    in_specs = (
        P(("groups", "hid"), "wid"),
        P(("groups", "wid"), "hid"),
        P(("groups", "wid"), "hid"),
        P(("groups", "wid"), "hid"),
        P(("groups", "hid"), "wid"),
        P(("groups", "hid"), "wid"),
    )
    out_specs = P(("groups", "hid"), "wid")
    return jax.shard_map(
        functools.partial(per_device, mesh.shape["hid"]),
        mesh=mesh, in_specs=in_specs, out_specs=out_specs, check_vma=False,
    )
```
